32 devices in a mesh: parts: 2 (over y), row: 16 (over z, x, core).
Axes of the slice: x: 2, y: 2, z: 4, core: 2. Of those that a mesh axis runs over, the one named last changes fastest.
Arguments:
- traces: bfloat16 [256, 2, 12000], P(('parts', 'row')), parts along dimension 0, may hold values from -160 to 160
- valid_mask: int32 [256, 2], P(('parts', 'row')), parts along dimension 0, may hold values 0 or 1
- pair_table: int32 [32, 10], P(('parts', 'row')), parts along dimension 0, may hold values from 0 to 15, as said below
- stack_in: float32 [32, 10, 8, 8, 401], P(('parts', 'row')), parts along dimension 0, may hold values from -6 to 6
Outputs:
- stacks: float32 [32, 10, 8, 8, 401], P(('parts', 'row')), parts along dimension 0
The draws below stay inside these ranges and needn't reach their ends.
There are 2 independent parts, one for each index of `parts`. The reference program is written for one: setup_inputs(seed, part) draws one part's arguments, and reference() takes and returns one part's arrays. A program takes and returns all parts, laid end to end along the dimension named above; each array names one. Nothing has to cross between parts.
Inputs may be any that keep to these rules, and one draw needn't show every extreme that they name: `pair_table`: row i lists the panels (i + k) mod 16 for k = -1 to 8, each once, in an order that varies from row to row.
All inputs are finite; a program needn't handle non-finite values. No bound on the sum of `valid_mask` on one device may be relied on, other than what follows from the above.
Results may differ from the reference program's by a relative error of at most 0.0032.
Values may be sent and summed in bfloat16 or wider, within the bound.
A program may use at most 128 MiB of HBM per device.

```python
import math
import jax
import jax.numpy as jnp
from jax import lax

CH_DEV = 8
SEGS = 2
SAMPLES = 12000
FLO = 6
BINS = 595
HALF = 40
LAGS = 401
CHANNELS = 128
OFFSETS = 10
N_ROW = 16


def draw_traces(key, part):
    base = jax.random.fold_in(key, 11)
    keys = jax.random.split(base, 5)
    noise = jax.random.truncated_normal(keys[0], -6.0, 6.0, (CHANNELS, SEGS, SAMPLES), jnp.float32)
    levels = jnp.exp(jax.random.uniform(keys[1], (CHANNELS, 1, 1), jnp.float32, 0.0, math.log(10.0)))
    tone_bins = jax.random.randint(keys[2], (CHANNELS, 4), FLO, FLO + BINS, dtype=jnp.int32)
    tone_sizes = jnp.exp(jax.random.uniform(keys[3], (CHANNELS, 4), jnp.float32, math.log(0.1), 0.0))
    tone_phase = jax.random.randint(keys[4], (CHANNELS, 4), 0, SAMPLES, dtype=jnp.int32)
    times = jnp.arange(SAMPLES, dtype=jnp.int32)
    signal = noise
    for number in range(4):
        index = (tone_bins[:, number, None] * times[None, :] + tone_phase[:, number, None]) % SAMPLES
        wave = tone_sizes[:, number, None] * jnp.sin(index.astype(jnp.float32) * (2.0 * math.pi / SAMPLES))
        signal = signal + wave[:, None, :]
    return (signal * levels).astype(jnp.bfloat16)


def draw_pair_table(key, part):
    base = jax.random.fold_in(key, 7)
    scores = jax.random.randint(base, (N_ROW, OFFSETS), 0, 1 << 20, dtype=jnp.int32) * OFFSETS
    scores = scores + jnp.arange(OFFSETS, dtype=jnp.int32)[None, :]
    order = jnp.argsort(scores, axis=1, stable=True).astype(jnp.int32)
    panels = jnp.arange(N_ROW, dtype=jnp.int32)[:, None]
    return ((panels + order - 1 + N_ROW) % N_ROW).astype(jnp.int32)


def set_ends(entries, key, least, largest):
    longest = entries.shape.index(max(entries.shape))
    spots = []
    for shift in (0, 1):
        where = [jax.random.randint(jax.random.fold_in(key, axis), (), 0, length) for axis, length in enumerate(entries.shape)]
        where[longest] = (where[longest] + shift) % entries.shape[longest]
        spots.append(tuple(where))
    return entries.at[spots[0]].set(least).at[spots[1]].set(largest)


def block_levels(own_key, dims, cuts, low, high):
    gain = 1.0
    for axis_at, shards_of in cuts:
        steps = jax.random.uniform(jax.random.fold_in(jax.random.fold_in(own_key, 6), axis_at), (shards_of,), jnp.float32, low / len(cuts), high / len(cuts))
        gain = gain * jnp.repeat(jnp.exp(steps), dims[axis_at] // shards_of).reshape((-1,) + (1,) * (len(dims) - 1 - axis_at))
    return gain


def normal_values(key, extent, width, limit, shards=(), kind=jnp.bfloat16):
    gain = block_levels(key, extent, shards, -0.22, 0.18) if shards else 1.0
    values = jax.random.normal(key, extent, jnp.float32) * width * gain
    return jnp.minimum(jnp.maximum(values, -limit), limit).astype(kind)


def setup_inputs(seed: int = 0, part: int = 0) -> dict:
    key_list = jax.random.split(jax.random.key(seed), 5)
    part_splits = jax.random.split(jax.random.fold_in(key_list[4], part), 5)
    return {
        "traces": draw_traces(jax.random.fold_in(jax.random.fold_in(key_list[4], part), 71), part),
        "valid_mask": set_ends((jax.random.randint(part_splits[1], (CHANNELS, SEGS), 0, 4) < 3).astype(jnp.int32), jax.random.fold_in(part_splits[1], 1), 0, 1),
        "pair_table": draw_pair_table(jax.random.fold_in(jax.random.fold_in(key_list[4], part), 71), part),
        "stack_in": normal_values(part_splits[3], (N_ROW, OFFSETS, CH_DEV, CH_DEV, LAGS), 1.0, 6.0, ((0, 16),), jnp.float32),
    }


epsilon = 1e-06

def spectra_of(rows, samples, first_bin, bins):
    length = samples // 8
    freq = first_bin + jnp.arange(bins, dtype=jnp.int32)

    def absorb(totals, block_index):
        first_row = block_index * length
        segment = lax.dynamic_slice_in_dim(rows, first_row, length, 1)
        times = first_row + jnp.arange(length, dtype=jnp.int32)
        angle = (times[:, None] * freq[None, :] % samples).astype(jnp.float32) * (2.0 * math.pi / samples)
        table = jnp.concatenate([jnp.cos(angle), -jnp.sin(angle)], axis=1).astype(jnp.bfloat16)
        return (totals + jnp.dot(segment, table, preferred_element_type=jnp.float32), None)
    start_total = jnp.zeros((rows.shape[0], 2 * bins), jnp.float32)
    totals, unused = lax.scan(absorb, start_total, jnp.arange(8, dtype=jnp.int32))
    return totals

def whiten_rows(traces, valid_mask, first_bin, bins, half_width):
    chans, minutes, samples = traces.shape
    spectrum = spectra_of(traces.reshape(chans * minutes, samples), samples, first_bin, bins)
    real_part = spectrum[:, :bins]
    imag_part = spectrum[:, bins:]
    power = real_part * real_part + imag_part * imag_part
    positions = jnp.arange(bins, dtype=jnp.int32)
    near = (jnp.abs(positions[:, None] - positions[None, :]) <= half_width).astype(jnp.float32)
    window = near / lax.optimization_barrier(jnp.sum(near, axis=0, keepdims=True))
    smooth = jnp.dot(power, window, precision=lax.Precision.HIGHEST)
    divisor = jnp.sqrt(smooth + epsilon)
    flags = valid_mask.reshape(-1, 1).astype(jnp.float32)
    whitened = spectrum * flags / jnp.concatenate([divisor, divisor], axis=1)
    return whitened.astype(jnp.bfloat16).reshape(chans, minutes, 2 * bins)

def lag_matrix(first_bin, bins, lags, samples):
    freq = first_bin + jnp.arange(bins, dtype=jnp.int32)
    shifts = jnp.arange(lags, dtype=jnp.int32) - (lags - 1) // 2
    angle = (freq[:, None] * shifts[None, :] % samples).astype(jnp.float32) * (2.0 * math.pi / samples)
    return jnp.concatenate([jnp.cos(angle), -jnp.sin(angle)], axis=0).astype(jnp.bfloat16)

def tile_corr(own_white, own_flags, partner_white, partner_flags, lag_table):
    bins = lag_table.shape[0] // 2
    own = own_white.astype(jnp.float32)
    partner = partner_white.astype(jnp.float32)
    shape = (partner.shape[0], own.shape[0], partner.shape[1], bins)
    real_sum = jnp.zeros(shape, jnp.float32)
    imag_sum = jnp.zeros(shape, jnp.float32)
    joint_sum = jnp.zeros(shape[:3], jnp.float32)
    for minute in range(own.shape[1]):
        own_real = own[:, minute, :bins][None, :, None, :]
        own_imag = own[:, minute, bins:][None, :, None, :]
        part_real = partner[:, :, minute, :bins][:, None, :, :]
        part_imag = partner[:, :, minute, bins:][:, None, :, :]
        real_sum = real_sum + (own_real * part_real + own_imag * part_imag)
        imag_sum = imag_sum + (own_imag * part_real - own_real * part_imag)
        own_valid = own_flags[:, minute].astype(jnp.float32)[None, :, None]
        part_valid = partner_flags[:, :, minute].astype(jnp.float32)[:, None, :]
        joint_sum = joint_sum + own_valid * part_valid
    inverse = 1.0 / jnp.maximum(joint_sum, 1.0)
    cross = (jnp.concatenate([real_sum, imag_sum], axis=-1) * inverse[..., None]).astype(jnp.bfloat16)
    corr = jnp.dot(cross.reshape(-1, 2 * bins), lag_table, preferred_element_type=jnp.float32) * (1.0 / math.sqrt(bins))
    return corr.reshape(shape[0], shape[1], shape[2], lag_table.shape[1])

def reference(traces, valid_mask, pair_table, stack_in):
    whitened = whiten_rows(traces, valid_mask, FLO, BINS, HALF)
    panels = whitened.reshape(N_ROW, CH_DEV, SEGS, 2 * BINS)
    panel_flags = valid_mask.reshape(N_ROW, CH_DEV, SEGS)
    lag_table = lag_matrix(FLO, BINS, LAGS, SAMPLES)

    def handle(panel_index):
        columns = pair_table[panel_index]
        partner = jnp.take(panels, columns, axis=0)
        partner_flags = jnp.take(panel_flags, columns, axis=0)
        corr = tile_corr(panels[panel_index], panel_flags[panel_index], partner, partner_flags, lag_table)
        return stack_in[panel_index] + corr
    return lax.map(handle, jnp.arange(N_ROW, dtype=jnp.int32))
```

```python
import functools
import math

import jax
import jax.numpy as jnp
import ml_dtypes
import numpy as np
from jax import lax
from jax.experimental import pallas as pl
from jax.experimental.pallas import tpu as pltpu
from jax.sharding import PartitionSpec as P

SAMPLES = 12000
FLO = 6
BINS = 595
HALF = 40
LAGS = 401
EPSILON = 1e-06

LANE = 128
BLOCKS = -(-BINS // LANE)
WIDTH = BLOCKS * LANE
CHUNK = 512
CHUNKS = -(-SAMPLES // CHUNK)
LAGS_PAD = 512

MESH = pl.DeviceIdType.MESH


def waves(steps):
    freq = FLO + np.arange(BINS, dtype=np.int64)
    angle = (steps[:, None] * freq[None, :] % SAMPLES) * (2.0 * math.pi / SAMPLES)
    pad = ((0, 0), (0, WIDTH - BINS))
    return np.pad(np.cos(angle), pad), np.pad(-np.sin(angle), pad)


def interleave(real_part, imag_part):
    rows = real_part.shape[0]
    both = np.stack(
        [real_part.reshape(rows, BLOCKS, LANE), imag_part.reshape(rows, BLOCKS, LANE)], axis=2
    )
    return both.reshape(rows, 2 * WIDTH)


def tables():
    dft = interleave(*waves(np.arange(CHUNK, dtype=np.int64))).astype(ml_dtypes.bfloat16)
    turn_real, turn_imag = waves(CHUNK * np.arange(CHUNKS, dtype=np.int64))
    turns = np.stack([turn_real, turn_imag]).astype(np.float32)
    spots = np.arange(WIDTH)
    inside = (spots[:, None] < BINS) & (spots[None, :] < BINS)
    near = (np.abs(spots[:, None] - spots[None, :]) <= HALF) & inside
    counts = np.maximum(near.sum(axis=0, keepdims=True), 1)
    band = near.astype(ml_dtypes.bfloat16)
    inverse = (1.0 / counts).astype(np.float32)
    lag_real, lag_imag = waves(np.arange(LAGS, dtype=np.int64) - (LAGS - 1) // 2)
    lag = np.pad(interleave(lag_real, lag_imag).T, ((0, 0), (0, LAGS_PAD - LAGS)))
    return dft, turns, band, inverse, lag.astype(ml_dtypes.bfloat16)


def spectrum_of(x_ref, dft_ref, turns_ref):
    pieces = []
    rows = x_ref.shape[0]
    for chunk in range(CHUNKS):
        first = chunk * CHUNK
        last = min(first + CHUNK, SAMPLES)
        piece = x_ref[:, first:last]
        if last - first < CHUNK:
            blank = jnp.zeros((rows, CHUNK - (last - first)), piece.dtype)
            piece = jnp.concatenate([piece, blank], axis=1)
        pieces.append(piece)
    signal = jnp.concatenate(pieces, axis=0)
    result = []
    for block in range(BLOCKS):
        lanes = slice(2 * LANE * block, 2 * LANE * (block + 1))
        part = jnp.dot(signal, dft_ref[:, lanes], preferred_element_type=jnp.float32)
        bins = slice(LANE * block, LANE * (block + 1))
        real_part = jnp.zeros((rows, LANE), jnp.float32)
        imag_part = jnp.zeros((rows, LANE), jnp.float32)
        for chunk in range(CHUNKS):
            own = part[rows * chunk : rows * (chunk + 1)]
            turn_real = turns_ref[0, chunk : chunk + 1, bins]
            turn_imag = turns_ref[1, chunk : chunk + 1, bins]
            real_part = real_part + (own[:, :LANE] * turn_real - own[:, LANE:] * turn_imag)
            imag_part = imag_part + (own[:, :LANE] * turn_imag + own[:, LANE:] * turn_real)
        result.append((real_part, imag_part))
    return result


def flag_column(mask_ref, rows):
    chans, segs = mask_ref.shape
    place = lax.broadcasted_iota(jnp.int32, (rows, LANE), 0)
    column = jnp.zeros((rows, LANE), jnp.float32)
    for seg in range(segs):
        for chan in range(chans):
            flag = mask_ref[chan, seg].astype(jnp.float32)
            column = jnp.where(place == seg * chans + chan, flag, column)
    return column


def whitened_blocks(mask_ref, x_ref, dft_ref, turns_ref, band_ref, inverse_ref):
    rows = x_ref.shape[0]
    spectrum = spectrum_of(x_ref, dft_ref, turns_ref)
    power = jnp.concatenate([re * re + im * im for re, im in spectrum], axis=1)
    high = power.astype(jnp.bfloat16)
    low = (power - high.astype(jnp.float32)).astype(jnp.bfloat16)
    sums = jnp.dot(
        jnp.concatenate([high, low], axis=0), band_ref[...], preferred_element_type=jnp.float32
    )
    smooth = (sums[:rows] + sums[rows:]) * inverse_ref[...]
    flags = flag_column(mask_ref, rows)
    scale = lax.rsqrt(smooth + EPSILON)
    result = []
    for block, (re, im) in enumerate(spectrum):
        factor = scale[:, LANE * block : LANE * (block + 1)] * flags
        real_part, imag_part = re * factor, im * factor
        if block == BLOCKS - 1:
            lane = lax.broadcasted_iota(jnp.int32, (rows, LANE), 1)
            real_part = jnp.where(lane == LANE - 1, flags, real_part)
        result.append((real_part, imag_part))
    return result


def exchange(
    panel_count, reach, mask_ref, x_ref, dft_ref, turns_ref, band_ref, inverse_ref,
    out_ref, send_sem, forward_sem, recv_sem,
):
    me = lax.axis_index("row")
    chips = panel_count // 2
    chip = me // 2
    core = lax.rem(me, 2)
    sibling = {"row": 2 * chip + 1 - core}

    def same_core(offset):
        return {"row": 2 * lax.rem(chip + offset + chips, chips) + core}

    barrier = pltpu.get_barrier_semaphore()
    for offset in range(1, chips):
        pl.semaphore_signal(barrier, inc=1, device_id=same_core(offset), device_id_type=MESH)
    pl.semaphore_signal(barrier, inc=1, device_id=sibling, device_id_type=MESH)

    blocks = whitened_blocks(mask_ref, x_ref, dft_ref, turns_ref, band_ref, inverse_ref)
    own = core + 1
    for block, (re, im) in enumerate(blocks):
        first = 2 * LANE * block
        out_ref[own, :, first : first + LANE] = re.astype(jnp.bfloat16)
        out_ref[own, :, first + LANE : first + 2 * LANE] = im.astype(jnp.bfloat16)

    pl.semaphore_wait(barrier, chips)

    def copy(source, target, sem, device):
        return pltpu.make_async_remote_copy(
            src_ref=out_ref.at[source],
            dst_ref=out_ref.at[target],
            send_sem=sem,
            recv_sem=recv_sem.at[target],
            device_id=device,
            device_id_type=MESH,
        )

    direct = [
        copy(own, 2 * step + core + 1, send_sem.at[step + 1], same_core(-step))
        for step in range(reach, 0, -1)
    ]
    back = copy(own, 0, send_sem.at[0], same_core(1))
    beside = copy(own, own, send_sem.at[1], sibling)
    for sent in direct:
        sent.start()

    @pl.when(core == 1)
    def _():
        back.start()

    beside.start()

    forwards = []
    back_forward = copy(0, 0, forward_sem.at[0], sibling)
    for step in range(1, reach + 1):
        slot = 2 * step + core + 1
        passed = copy(slot, slot, forward_sem.at[step], sibling)
        passed.wait_recv()
        passed.start()
        forwards.append(passed)
        if step == 1:

            @pl.when(core == 1)
            def _():
                back_forward.wait_recv()
                back_forward.start()

    copy(2 - core, 2 - core, send_sem.at[1], sibling).wait_recv()
    for step in range(1, reach + 1):
        slot = 2 * step + 2 - core
        copy(slot, slot, forward_sem.at[step], sibling).wait_recv()

    @pl.when(core == 0)
    def _():
        back_forward.wait_recv()

    for sent in direct + [beside] + forwards:
        sent.wait_send()

    @pl.when(core == 1)
    def _():
        back.wait_send()
        back_forward.wait_send()


def correlate(panel_count, pair_ref, panels_ref, lag_ref, stack_ref, out_ref, cross_ref):
    me = lax.axis_index("row")
    core = lax.rem(me, 2)
    first = me - core - 1
    step = pl.program_id(0)
    slots = stack_ref.shape[1]
    chans = stack_ref.shape[2]
    own = panels_ref[core + 1].astype(jnp.float32)
    segs = own.shape[0] // chans
    for slot in range(slots):
        panel = pair_ref[0, step * slots + slot]
        place = lax.rem(panel - first + panel_count, panel_count)
        partner = panels_ref[place].astype(jnp.float32)
        for chan in range(chans):
            scale = None
            for block in range(BLOCKS - 1, -1, -1):
                at = 2 * LANE * block
                re = im = 0.0
                for seg in range(segs):
                    mine = own[seg * chans + chan : seg * chans + chan + 1]
                    other = partner[seg * chans : (seg + 1) * chans]
                    own_re, own_im = mine[:, at : at + LANE], mine[:, at + LANE : at + 2 * LANE]
                    part_re, part_im = other[:, at : at + LANE], other[:, at + LANE : at + 2 * LANE]
                    re = re + (own_re * part_re + own_im * part_im)
                    im = im + (own_im * part_re - own_re * part_im)
                if scale is None:
                    count = re[:, LANE - 1 : LANE]
                    scale = 1.0 / jnp.maximum(count, 1.0)
                row = (slot * chans + chan) * chans
                cross_ref[row : row + chans, at : at + LANE] = (re * scale).astype(jnp.bfloat16)
                cross_ref[row : row + chans, at + LANE : at + 2 * LANE] = (im * scale).astype(
                    jnp.bfloat16
                )
    corr = jnp.dot(cross_ref[...], lag_ref[...], preferred_element_type=jnp.float32)
    corr = corr[:, :LAGS] * (1.0 / math.sqrt(BINS))
    out_ref[...] = stack_ref[...] + corr.reshape(stack_ref.shape)


def shards(traces, valid_mask, pair_table, stack_in):
    panel_count = lax.axis_size("row")
    chans, segs, samples = traces.shape
    rows = chans * segs
    offsets = pair_table.shape[1]
    reach = (offsets - 2) // 2
    dft, turns, band, inverse, lag = tables()
    x = jnp.transpose(traces, (1, 0, 2)).reshape(rows, samples)
    vmem = pl.BlockSpec(memory_space=pltpu.VMEM)
    smem = pl.BlockSpec(memory_space=pltpu.SMEM)
    panels = pl.pallas_call(
        functools.partial(exchange, panel_count, reach),
        out_shape=jax.ShapeDtypeStruct((offsets + 1, rows, 2 * WIDTH), jnp.bfloat16),
        in_specs=[smem] + [vmem] * 5,
        out_specs=vmem,
        scratch_shapes=[
            pltpu.SemaphoreType.DMA((reach + 2,)),
            pltpu.SemaphoreType.DMA((reach + 2,)),
            pltpu.SemaphoreType.DMA((offsets + 1,)),
        ],
        compiler_params=pltpu.CompilerParams(
            collective_id=0, has_side_effects=True, vmem_limit_bytes=32 << 20
        ),
    )(valid_mask, x, jnp.asarray(dft), jnp.asarray(turns), jnp.asarray(band), jnp.asarray(inverse))
    group = max(size for size in range(1, 7) if offsets % size == 0)
    tile = (1, group, chans, chans, stack_in.shape[4])
    return pl.pallas_call(
        functools.partial(correlate, panel_count),
        out_shape=jax.ShapeDtypeStruct(stack_in.shape, stack_in.dtype),
        grid_spec=pltpu.PrefetchScalarGridSpec(
            num_scalar_prefetch=1,
            grid=(offsets // group,),
            in_specs=[
                pl.BlockSpec(panels.shape, lambda i, pair: (0, 0, 0)),
                pl.BlockSpec(lag.shape, lambda i, pair: (0, 0)),
                pl.BlockSpec(tile, lambda i, pair: (0, i, 0, 0, 0)),
            ],
            out_specs=pl.BlockSpec(tile, lambda i, pair: (0, i, 0, 0, 0)),
            scratch_shapes=[pltpu.VMEM((group * chans * chans, 2 * WIDTH), jnp.bfloat16)],
        ),
        compiler_params=pltpu.CompilerParams(vmem_limit_bytes=32 << 20),
    )(pair_table, panels, jnp.asarray(lag), stack_in)


def solution(mesh):
    in_specs = (
        P(("parts", "row"), None, None),
        P(("parts", "row"), None),
        P(("parts", "row"), None),
        P(("parts", "row"), None, None, None, None),
    )
    out_specs = P(("parts", "row"), None, None, None, None)
    return jax.shard_map(shards, mesh=mesh, in_specs=in_specs, out_specs=out_specs, check_vma=False)
```

```python
import functools
import math

import jax
import jax.numpy as jnp
import ml_dtypes
import numpy as np
from jax import lax
from jax.experimental import pallas as pl
from jax.experimental.pallas import tpu as pltpu
from jax.sharding import PartitionSpec as P

SAMPLES = 12000
FLO = 6
BINS = 595
HALF = 40
LAGS = 401
EPSILON = 1e-06

LANE = 128
BLOCKS = -(-BINS // LANE)
WIDTH = BLOCKS * LANE
CHUNK = 512
CHUNKS = -(-SAMPLES // CHUNK)
LAGS_PAD = 512

MESH = pl.DeviceIdType.MESH


def waves(steps):
    freq = FLO + np.arange(BINS, dtype=np.int64)
    angle = (steps[:, None] * freq[None, :] % SAMPLES) * (2.0 * math.pi / SAMPLES)
    pad = ((0, 0), (0, WIDTH - BINS))
    return np.pad(np.cos(angle), pad), np.pad(-np.sin(angle), pad)


def interleave(real_part, imag_part):
    rows = real_part.shape[0]
    both = np.stack(
        [real_part.reshape(rows, BLOCKS, LANE), imag_part.reshape(rows, BLOCKS, LANE)], axis=2
    )
    return both.reshape(rows, 2 * WIDTH)


def tables():
    dft = interleave(*waves(np.arange(CHUNK, dtype=np.int64))).astype(ml_dtypes.bfloat16)
    turn_real, turn_imag = waves(CHUNK * np.arange(CHUNKS, dtype=np.int64))
    spots = np.arange(WIDTH)
    inside = (spots[:, None] < BINS) & (spots[None, :] < BINS)
    near = (np.abs(spots[:, None] - spots[None, :]) <= HALF) & inside
    counts = np.maximum(near.sum(axis=0, keepdims=True), 1)
    band = near.astype(ml_dtypes.bfloat16)
    turns = np.concatenate([turn_real, turn_imag, 1.0 / counts], axis=0)
    turns = np.pad(turns, ((0, -turns.shape[0] % 8), (0, 0))).astype(np.float32)
    lag_real, lag_imag = waves(np.arange(LAGS, dtype=np.int64) - (LAGS - 1) // 2)
    lag = np.pad(interleave(lag_real, lag_imag).T, ((0, 0), (0, LAGS_PAD - LAGS)))
    return dft, turns, band, lag.astype(ml_dtypes.bfloat16)


def spectrum_of(x_ref, dft_ref, turns_ref, ready):
    pieces = []
    chans, segs = x_ref.shape[:2]
    rows = chans * segs
    for chunk in range(CHUNKS):
        first = chunk * CHUNK
        last = min(first + CHUNK, SAMPLES)
        piece = x_ref[:, :, first:last].reshape(rows, last - first)
        if last - first < CHUNK:
            blank = jnp.zeros((rows, CHUNK - (last - first)), piece.dtype)
            piece = jnp.concatenate([piece, blank], axis=1)
        pieces.append(piece)
    signal = jnp.concatenate(pieces, axis=0)
    result = []
    for block in range(BLOCKS):
        ready(block)
        lanes = slice(2 * LANE * block, 2 * LANE * (block + 1))
        part = jnp.dot(signal, dft_ref[:, lanes], preferred_element_type=jnp.float32)
        bins = slice(LANE * block, LANE * (block + 1))
        real_part = jnp.zeros((rows, LANE), jnp.float32)
        imag_part = jnp.zeros((rows, LANE), jnp.float32)
        for chunk in range(CHUNKS):
            own = part[rows * chunk : rows * (chunk + 1)]
            turn_real = turns_ref[chunk : chunk + 1, bins]
            turn_imag = turns_ref[CHUNKS + chunk : CHUNKS + chunk + 1, bins]
            real_part = real_part + (own[:, :LANE] * turn_real - own[:, LANE:] * turn_imag)
            imag_part = imag_part + (own[:, :LANE] * turn_imag + own[:, LANE:] * turn_real)
        result.append((real_part, imag_part))
    return result


def flag_column(mask_ref, rows):
    segs, chans = mask_ref.shape
    place = lax.broadcasted_iota(jnp.int32, (rows, LANE), 0)
    column = jnp.zeros((rows, LANE), jnp.float32)
    for seg in range(segs):
        for chan in range(chans):
            flag = mask_ref[seg, chan].astype(jnp.float32)
            column = jnp.where(place == chan * segs + seg, flag, column)
    return column


def whitened_blocks(mask_ref, x_ref, dft_ref, turns_ref, band_ref, ready, band_ready):
    rows = x_ref.shape[0] * x_ref.shape[1]
    spectrum = spectrum_of(x_ref, dft_ref, turns_ref, ready)
    band_ready()
    power = jnp.concatenate([re * re + im * im for re, im in spectrum], axis=1)
    high = power.astype(jnp.bfloat16)
    low = (power - high.astype(jnp.float32)).astype(jnp.bfloat16)
    sums = jnp.dot(
        jnp.concatenate([high, low], axis=0), band_ref[...], preferred_element_type=jnp.float32
    )
    smooth = (sums[:rows] + sums[rows:]) * turns_ref[2 * CHUNKS : 2 * CHUNKS + 1]
    flags = flag_column(mask_ref, rows)
    scale = lax.rsqrt(smooth + EPSILON)
    result = []
    for block, (re, im) in enumerate(spectrum):
        factor = scale[:, LANE * block : LANE * (block + 1)] * flags
        real_part, imag_part = re * factor, im * factor
        if block == BLOCKS - 1:
            lane = lax.broadcasted_iota(jnp.int32, (rows, LANE), 1)
            real_part = jnp.where(lane == LANE - 1, flags, real_part)
        result.append((real_part, imag_part))
    return result


def kernel(
    panel_count, mask_ref, pair_ref, x_hbm, dft_hbm, turns_hbm, band_hbm, lag_hbm, stack_hbm,
    out_ref, x_ref, dft_ref, turns_ref, band_ref, lag_ref, stack_ref, white_ref, panels_ref,
    cross_ref, corr_ref, load_sem, send_sem, forward_sem, recv_sem,
):
    offsets, chans = stack_ref.shape[:2]
    segs = x_ref.shape[1]
    reach = (offsets - 2) // 2
    loads = [
        pltpu.make_async_copy(x_hbm, x_ref, load_sem.at[0]),
        pltpu.make_async_copy(turns_hbm, turns_ref, load_sem.at[1]),
    ]
    for block in range(BLOCKS):
        lanes = pl.ds(2 * LANE * block, 2 * LANE)
        loads.append(
            pltpu.make_async_copy(
                dft_hbm.at[:, lanes], dft_ref.at[:, lanes], load_sem.at[2 + block]
            )
        )
    loads.append(pltpu.make_async_copy(band_hbm, band_ref, load_sem.at[2 + BLOCKS]))
    late_loads = [
        pltpu.make_async_copy(lag_hbm, lag_ref, load_sem.at[3 + BLOCKS]),
        pltpu.make_async_copy(stack_hbm.at[0], stack_ref, load_sem.at[4 + BLOCKS]),
    ]
    for load in loads + late_loads:
        load.start()

    me = lax.axis_index("row")
    chips = panel_count // 2
    chip = me // 2
    core = lax.rem(me, 2)
    sibling = {"row": 2 * chip + 1 - core}

    def same_core(offset):
        return {"row": 2 * lax.rem(chip + offset + chips, chips) + core}

    barrier = pltpu.get_barrier_semaphore()
    for offset in range(1, chips):
        pl.semaphore_signal(barrier, inc=1, device_id=same_core(offset), device_id_type=MESH)
    pl.semaphore_signal(barrier, inc=1, device_id=sibling, device_id_type=MESH)

    loads[0].wait()
    loads[1].wait()
    blocks = whitened_blocks(
        mask_ref, x_ref, dft_ref, turns_ref, band_ref,
        lambda block: loads[2 + block].wait(), loads[2 + BLOCKS].wait,
    )
    own = core + 1
    for place, part in enumerate(part for pair in blocks for part in pair):
        white_ref[place] = part
        ordered = [white_ref[place, pl.ds(seg, chans, stride=segs), :] for seg in range(segs)]
        panels_ref[own, :, LANE * place : LANE * (place + 1)] = jnp.concatenate(
            ordered, axis=0
        ).astype(jnp.bfloat16)

    pl.semaphore_wait(barrier, chips)

    def copy(source, target, sem, device):
        return pltpu.make_async_remote_copy(
            src_ref=panels_ref.at[source],
            dst_ref=panels_ref.at[target],
            send_sem=sem,
            recv_sem=recv_sem.at[target],
            device_id=device,
            device_id_type=MESH,
        )

    direct = [
        copy(own, 2 * step + core + 1, send_sem.at[step + 1], same_core(-step))
        for step in range(1, reach + 1)
    ]
    back = copy(own, 0, send_sem.at[0], same_core(1))
    beside = copy(own, own, send_sem.at[1], sibling)
    beside.start()
    for sent in direct:
        sent.start()

    @pl.when(core == 1)
    def _():
        back.start()

    def correlate(slots):
        mine = panels_ref[own].astype(jnp.float32)
        for index, slot in enumerate(slots):
            partner = panels_ref[slot].astype(jnp.float32)
            scales = [None] * chans
            for block in range(BLOCKS - 1, -1, -1):
                at = 2 * LANE * block
                cut_re, cut_im = slice(at, at + LANE), slice(at + LANE, at + 2 * LANE)
                real_rows, imag_rows = [], []
                for chan in range(chans):
                    re = im = 0.0
                    for seg in range(segs):
                        row = slice(seg * chans + chan, seg * chans + chan + 1)
                        other = slice(seg * chans, (seg + 1) * chans)
                        own_re, own_im = mine[row, cut_re], mine[row, cut_im]
                        part_re, part_im = partner[other, cut_re], partner[other, cut_im]
                        re = re + (own_re * part_re + own_im * part_im)
                        im = im + (own_im * part_re - own_re * part_im)
                    if scales[chan] is None:
                        scales[chan] = 1.0 / jnp.maximum(re[:, LANE - 1 : LANE], 1.0)
                    real_rows.append(re * scales[chan])
                    imag_rows.append(im * scales[chan])
                rows = slice(index * chans * chans, (index + 1) * chans * chans)
                cross_ref[rows, cut_re] = jnp.concatenate(real_rows, axis=0).astype(jnp.bfloat16)
                cross_ref[rows, cut_im] = jnp.concatenate(imag_rows, axis=0).astype(jnp.bfloat16)
        corr = jnp.dot(cross_ref[...], lag_ref[...], preferred_element_type=jnp.float32)
        corr = corr[:, :LAGS] * (1.0 / math.sqrt(BINS))
        for index, slot in enumerate(slots):
            corr_ref[slot] = corr[index * chans * chans : (index + 1) * chans * chans]

    copy(2 - core, 2 - core, send_sem.at[1], sibling).wait_recv()
    for load in late_loads:
        load.wait()
    correlate([1, 2])

    def forward(slot, step):
        return copy(slot, slot, forward_sem.at[step], sibling)

    def arrive(step, carry):
        passed = forward(2 * step + core + 1, step)
        passed.wait_recv()
        passed.start()
        forward(2 * step + 2 - core, step).wait_recv()
        correlate([2 * step + 1, 2 * step + 2])
        return carry

    lax.fori_loop(1, reach, arrive, 0)

    far = 2 * reach + 1
    passed = forward(far * (1 - core), reach)
    passed.wait_recv()
    passed.start()

    @pl.when(core == 1)
    def _():
        copy(far + 1, far + 1, send_sem.at[0], sibling).wait_recv()

    forward(far * core, reach).wait_recv()
    correlate([far, (far + 1) * core])

    first = me - core - 1

    def accumulate(slot, carry):
        place = lax.rem(pair_ref[0, slot] - first + panel_count, panel_count)
        place = jnp.clip(place, 0, offsets)
        out_ref[0, slot] = stack_ref[slot] + corr_ref[place].reshape(stack_ref.shape[1:])
        return carry

    lax.fori_loop(0, offsets, accumulate, 0, unroll=2)

    for sent in direct + [beside]:
        sent.wait_send()

    def forwarded(step, carry):
        forward(own, step).wait_send()
        return carry

    lax.fori_loop(1, reach + 1, forwarded, 0)

    @pl.when(core == 1)
    def _():
        back.wait_send()


def shards(traces, valid_mask, pair_table, stack_in):
    panel_count = lax.axis_size("row")
    chans, segs, samples = traces.shape
    rows = chans * segs
    offsets = pair_table.shape[1]
    reach = (offsets - 2) // 2
    dft, turns, band, lag = tables()
    vmem = pl.BlockSpec(memory_space=pltpu.VMEM)
    hbm = pl.BlockSpec(memory_space=pltpu.HBM)
    smem = pl.BlockSpec(memory_space=pltpu.SMEM)
    return pl.pallas_call(
        functools.partial(kernel, panel_count),
        out_shape=jax.ShapeDtypeStruct(stack_in.shape, stack_in.dtype),
        in_specs=[smem] * 2 + [hbm] * 6,
        out_specs=vmem,
        scratch_shapes=[
            pltpu.VMEM(traces.shape, traces.dtype),
            pltpu.VMEM(dft.shape, jnp.bfloat16),
            pltpu.VMEM(turns.shape, jnp.float32),
            pltpu.VMEM(band.shape, jnp.bfloat16),
            pltpu.VMEM(lag.shape, jnp.bfloat16),
            pltpu.VMEM(stack_in.shape[1:], jnp.float32),
            pltpu.VMEM((2 * BLOCKS, rows, LANE), jnp.float32),
            pltpu.VMEM((offsets + 1, rows, 2 * WIDTH), jnp.bfloat16),
            pltpu.VMEM((2 * chans * chans, 2 * WIDTH), jnp.bfloat16),
            pltpu.VMEM((offsets + 1, chans * chans, LAGS), jnp.float32),
            pltpu.SemaphoreType.DMA((5 + BLOCKS,)),
            pltpu.SemaphoreType.DMA((reach + 2,)),
            pltpu.SemaphoreType.DMA((reach + 1,)),
            pltpu.SemaphoreType.DMA((offsets + 1,)),
        ],
        compiler_params=pltpu.CompilerParams(
            collective_id=0, has_side_effects=True, vmem_limit_bytes=56 << 20
        ),
    )(
        valid_mask.T, pair_table, traces, jnp.asarray(dft), jnp.asarray(turns),
        jnp.asarray(band), jnp.asarray(lag), stack_in,
    )


def solution(mesh):
    in_specs = (
        P(("parts", "row"), None, None),
        P(("parts", "row"), None),
        P(("parts", "row"), None),
        P(("parts", "row"), None, None, None, None),
    )
    out_specs = P(("parts", "row"), None, None, None, None)
    return jax.shard_map(shards, mesh=mesh, in_specs=in_specs, out_specs=out_specs, check_vma=False)
```

```python
import functools
import math

import jax
import jax.numpy as jnp
import ml_dtypes
import numpy as np
from jax import lax
from jax.experimental import pallas as pl
from jax.experimental.pallas import tpu as pltpu
from jax.sharding import PartitionSpec as P

SAMPLES = 12000
FLO = 6
BINS = 595
HALF = 40
LAGS = 401
EPSILON = 1e-06

LANE = 128
BLOCKS = -(-BINS // LANE)
WIDTH = BLOCKS * LANE
CHUNK = 512
CHUNKS = -(-SAMPLES // CHUNK)
LAGS_PAD = 512

MESH = pl.DeviceIdType.MESH


def waves(steps):
    freq = FLO + np.arange(BINS, dtype=np.int64)
    angle = (steps[:, None] * freq[None, :] % SAMPLES) * (2.0 * math.pi / SAMPLES)
    pad = ((0, 0), (0, WIDTH - BINS))
    return np.pad(np.cos(angle), pad), np.pad(-np.sin(angle), pad)


def interleave(real_part, imag_part):
    rows = real_part.shape[0]
    both = np.stack(
        [real_part.reshape(rows, BLOCKS, LANE), imag_part.reshape(rows, BLOCKS, LANE)], axis=2
    )
    return both.reshape(rows, 2 * WIDTH)


def tables():
    dft = interleave(*waves(np.arange(CHUNK, dtype=np.int64))).astype(ml_dtypes.bfloat16)
    turn_real, turn_imag = waves(CHUNK * np.arange(CHUNKS, dtype=np.int64))
    spots = np.arange(WIDTH)
    inside = (spots[:, None] < BINS) & (spots[None, :] < BINS)
    near = (np.abs(spots[:, None] - spots[None, :]) <= HALF) & inside
    counts = np.maximum(near.sum(axis=0, keepdims=True), 1)
    band = near.astype(ml_dtypes.bfloat16)
    turns = np.concatenate([turn_real, turn_imag, 1.0 / counts], axis=0)
    turns = np.pad(turns, ((0, -turns.shape[0] % 8), (0, 0))).astype(np.float32)
    lag_real, lag_imag = waves(np.arange(LAGS, dtype=np.int64) - (LAGS - 1) // 2)
    lag = np.pad(interleave(lag_real, lag_imag).T, ((0, 0), (0, LAGS_PAD - LAGS)))
    return dft, turns, band, lag.astype(ml_dtypes.bfloat16)


def spectrum_of(x_ref, dft_ref, turns_ref, ready):
    pieces = []
    chans, segs = x_ref.shape[:2]
    rows = chans * segs
    for chunk in range(CHUNKS):
        first = chunk * CHUNK
        last = min(first + CHUNK, SAMPLES)
        piece = x_ref[:, :, first:last].reshape(rows, last - first)
        if last - first < CHUNK:
            blank = jnp.zeros((rows, CHUNK - (last - first)), piece.dtype)
            piece = jnp.concatenate([piece, blank], axis=1)
        pieces.append(piece)
    signal = jnp.concatenate(pieces, axis=0)
    result = []
    for block in range(BLOCKS):
        ready(block)
        lanes = slice(2 * LANE * block, 2 * LANE * (block + 1))
        part = jnp.dot(signal, dft_ref[:, lanes], preferred_element_type=jnp.float32)
        bins = slice(LANE * block, LANE * (block + 1))
        real_part = jnp.zeros((rows, LANE), jnp.float32)
        imag_part = jnp.zeros((rows, LANE), jnp.float32)
        for chunk in range(CHUNKS):
            own = part[rows * chunk : rows * (chunk + 1)]
            turn_real = turns_ref[chunk : chunk + 1, bins]
            turn_imag = turns_ref[CHUNKS + chunk : CHUNKS + chunk + 1, bins]
            real_part = real_part + (own[:, :LANE] * turn_real - own[:, LANE:] * turn_imag)
            imag_part = imag_part + (own[:, :LANE] * turn_imag + own[:, LANE:] * turn_real)
        result.append((real_part, imag_part))
    return result


def flag_column(mask_ref, rows):
    segs, chans = mask_ref.shape
    place = lax.broadcasted_iota(jnp.int32, (rows, LANE), 0)
    column = jnp.zeros((rows, LANE), jnp.float32)
    for seg in range(segs):
        for chan in range(chans):
            flag = mask_ref[seg, chan].astype(jnp.float32)
            column = jnp.where(place == chan * segs + seg, flag, column)
    return column


def whitened_blocks(mask_ref, x_ref, dft_ref, turns_ref, band_ref, ready, band_ready):
    rows = x_ref.shape[0] * x_ref.shape[1]
    spectrum = spectrum_of(x_ref, dft_ref, turns_ref, ready)
    band_ready()
    power = jnp.concatenate([re * re + im * im for re, im in spectrum], axis=1)
    high = power.astype(jnp.bfloat16)
    low = (power - high.astype(jnp.float32)).astype(jnp.bfloat16)
    sums = jnp.dot(
        jnp.concatenate([high, low], axis=0), band_ref[...], preferred_element_type=jnp.float32
    )
    smooth = (sums[:rows] + sums[rows:]) * turns_ref[2 * CHUNKS : 2 * CHUNKS + 1]
    flags = flag_column(mask_ref, rows)
    scale = lax.rsqrt(smooth + EPSILON)
    result = []
    for block, (re, im) in enumerate(spectrum):
        factor = scale[:, LANE * block : LANE * (block + 1)] * flags
        real_part, imag_part = re * factor, im * factor
        if block == BLOCKS - 1:
            lane = lax.broadcasted_iota(jnp.int32, (rows, LANE), 1)
            real_part = jnp.where(lane == LANE - 1, flags, real_part)
        result.append((real_part, imag_part))
    return result


def exchange(
    panel_count, reach, mask_ref, x_hbm, dft_hbm, turns_hbm, band_hbm,
    out_ref, x_ref, dft_ref, turns_ref, band_ref, white_ref, load_sem,
    send_sem, forward_sem, recv_sem,
):
    loads = [
        pltpu.make_async_copy(x_hbm, x_ref, load_sem.at[0]),
        pltpu.make_async_copy(turns_hbm, turns_ref, load_sem.at[1]),
    ]
    for block in range(BLOCKS):
        lanes = pl.ds(2 * LANE * block, 2 * LANE)
        loads.append(
            pltpu.make_async_copy(
                dft_hbm.at[:, lanes], dft_ref.at[:, lanes], load_sem.at[2 + block]
            )
        )
    loads.append(pltpu.make_async_copy(band_hbm, band_ref, load_sem.at[2 + BLOCKS]))
    for load in loads:
        load.start()

    me = lax.axis_index("row")
    chips = panel_count // 2
    chip = me // 2
    core = lax.rem(me, 2)
    sibling = {"row": 2 * chip + 1 - core}

    def same_core(offset):
        return {"row": 2 * lax.rem(chip + offset + chips, chips) + core}

    barrier = pltpu.get_barrier_semaphore()
    for offset in range(1, chips):
        pl.semaphore_signal(barrier, inc=1, device_id=same_core(offset), device_id_type=MESH)
    pl.semaphore_signal(barrier, inc=1, device_id=sibling, device_id_type=MESH)

    loads[0].wait()
    loads[1].wait()
    blocks = whitened_blocks(
        mask_ref, x_ref, dft_ref, turns_ref, band_ref,
        lambda block: loads[2 + block].wait(), loads[2 + BLOCKS].wait,
    )
    own = core + 1
    chans, segs = x_ref.shape[:2]
    for place, part in enumerate(part for pair in blocks for part in pair):
        white_ref[place] = part
        ordered = [white_ref[place, pl.ds(seg, chans, stride=segs), :] for seg in range(segs)]
        out_ref[own, :, LANE * place : LANE * (place + 1)] = jnp.concatenate(
            ordered, axis=0
        ).astype(jnp.bfloat16)

    pl.semaphore_wait(barrier, chips)

    def copy(source, target, sem, device):
        return pltpu.make_async_remote_copy(
            src_ref=out_ref.at[source],
            dst_ref=out_ref.at[target],
            send_sem=sem,
            recv_sem=recv_sem.at[target],
            device_id=device,
            device_id_type=MESH,
        )

    direct = [
        copy(own, 2 * step + core + 1, send_sem.at[step + 1], same_core(-step))
        for step in range(reach, 0, -1)
    ]
    back = copy(own, 0, send_sem.at[0], same_core(1))
    beside = copy(own, own, send_sem.at[1], sibling)
    for sent in direct:
        sent.start()

    @pl.when(core == 1)
    def _():
        back.start()

    beside.start()

    forwards = []
    back_forward = copy(0, 0, forward_sem.at[0], sibling)
    for step in range(1, reach + 1):
        slot = 2 * step + core + 1
        passed = copy(slot, slot, forward_sem.at[step], sibling)
        passed.wait_recv()
        passed.start()
        forwards.append(passed)
        if step == 1:

            @pl.when(core == 1)
            def _():
                back_forward.wait_recv()
                back_forward.start()

    copy(2 - core, 2 - core, send_sem.at[1], sibling).wait_recv()
    for step in range(1, reach + 1):
        slot = 2 * step + 2 - core
        copy(slot, slot, forward_sem.at[step], sibling).wait_recv()

    @pl.when(core == 0)
    def _():
        back_forward.wait_recv()

    for sent in direct + [beside] + forwards:
        sent.wait_send()

    @pl.when(core == 1)
    def _():
        back.wait_send()
        back_forward.wait_send()


def correlate(
    panel_count, group, pair_ref, panels_hbm, lag_hbm, stack_hbm, out_hbm,
    panels_ref, lag_ref, stack_ref, cross_ref, load_sem, out_sem,
):
    offsets, chans = stack_ref.shape[:2]
    loads = [
        pltpu.make_async_copy(panels_hbm, panels_ref, load_sem.at[0]),
        pltpu.make_async_copy(lag_hbm, lag_ref, load_sem.at[1]),
        pltpu.make_async_copy(stack_hbm.at[0], stack_ref, load_sem.at[2]),
    ]
    for load in loads:
        load.start()
    me = lax.axis_index("row")
    core = lax.rem(me, 2)
    first = me - core - 1
    loads[0].wait()
    own = panels_ref[core + 1].astype(jnp.float32)
    segs = own.shape[0] // chans

    def result(step):
        slots = pl.ds(step * group, group)
        return pltpu.make_async_copy(
            stack_ref.at[slots], out_hbm.at[0, slots], out_sem.at[step]
        )

    def advance(step, carry):
        for slot in range(group):
            panel = pair_ref[0, step * group + slot]
            place = lax.rem(panel - first + panel_count, panel_count)
            partner = panels_ref[jnp.clip(place, 0, offsets)].astype(jnp.float32)
            scales = [None] * chans
            for block in range(BLOCKS - 1, -1, -1):
                at = 2 * LANE * block
                cut_re, cut_im = slice(at, at + LANE), slice(at + LANE, at + 2 * LANE)
                real_rows, imag_rows = [], []
                for chan in range(chans):
                    re = im = 0.0
                    for seg in range(segs):
                        row = slice(seg * chans + chan, seg * chans + chan + 1)
                        other = slice(seg * chans, (seg + 1) * chans)
                        own_re, own_im = own[row, cut_re], own[row, cut_im]
                        part_re, part_im = partner[other, cut_re], partner[other, cut_im]
                        re = re + (own_re * part_re + own_im * part_im)
                        im = im + (own_im * part_re - own_re * part_im)
                    if scales[chan] is None:
                        scales[chan] = 1.0 / jnp.maximum(re[:, LANE - 1 : LANE], 1.0)
                    real_rows.append(re * scales[chan])
                    imag_rows.append(im * scales[chan])
                rows = slice(slot * chans * chans, (slot + 1) * chans * chans)
                cross_ref[rows, cut_re] = jnp.concatenate(real_rows, axis=0).astype(jnp.bfloat16)
                cross_ref[rows, cut_im] = jnp.concatenate(imag_rows, axis=0).astype(jnp.bfloat16)

        @pl.when(step == 0)
        def _():
            loads[1].wait()
            loads[2].wait()

        corr = jnp.dot(cross_ref[...], lag_ref[...], preferred_element_type=jnp.float32)
        corr = corr[:, :LAGS] * (1.0 / math.sqrt(BINS))
        slots = pl.ds(step * group, group)
        stack_ref[slots] = stack_ref[slots] + corr.reshape((group,) + stack_ref.shape[1:])
        result(step).start()
        return carry

    lax.fori_loop(0, offsets // group, advance, 0)

    def finish(step, carry):
        result(step).wait()
        return carry

    lax.fori_loop(0, offsets // group, finish, 0)


def shards(traces, valid_mask, pair_table, stack_in):
    panel_count = lax.axis_size("row")
    chans, segs, samples = traces.shape
    rows = chans * segs
    offsets = pair_table.shape[1]
    reach = (offsets - 2) // 2
    dft, turns, band, lag = tables()
    vmem = pl.BlockSpec(memory_space=pltpu.VMEM)
    hbm = pl.BlockSpec(memory_space=pltpu.HBM)
    smem = pl.BlockSpec(memory_space=pltpu.SMEM)
    panels = pl.pallas_call(
        functools.partial(exchange, panel_count, reach),
        out_shape=jax.ShapeDtypeStruct((offsets + 1, rows, 2 * WIDTH), jnp.bfloat16),
        in_specs=[smem] + [hbm] * 4,
        out_specs=vmem,
        scratch_shapes=[
            pltpu.VMEM(traces.shape, traces.dtype),
            pltpu.VMEM(dft.shape, jnp.bfloat16),
            pltpu.VMEM(turns.shape, jnp.float32),
            pltpu.VMEM(band.shape, jnp.bfloat16),
            pltpu.VMEM((2 * BLOCKS, rows, LANE), jnp.float32),
            pltpu.SemaphoreType.DMA((3 + BLOCKS,)),
            pltpu.SemaphoreType.DMA((reach + 2,)),
            pltpu.SemaphoreType.DMA((reach + 2,)),
            pltpu.SemaphoreType.DMA((offsets + 1,)),
        ],
        compiler_params=pltpu.CompilerParams(
            collective_id=0, has_side_effects=True, vmem_limit_bytes=60 << 20
        ),
    )(valid_mask.T, traces, jnp.asarray(dft), jnp.asarray(turns), jnp.asarray(band))
    group = max(size for size in range(1, 7) if offsets % size == 0)
    return pl.pallas_call(
        functools.partial(correlate, panel_count, group),
        out_shape=jax.ShapeDtypeStruct(stack_in.shape, stack_in.dtype),
        in_specs=[smem] + [hbm] * 3,
        out_specs=hbm,
        scratch_shapes=[
            pltpu.VMEM(panels.shape, panels.dtype),
            pltpu.VMEM(lag.shape, jnp.bfloat16),
            pltpu.VMEM(stack_in.shape[1:], jnp.float32),
            pltpu.VMEM((group * chans * chans, 2 * WIDTH), jnp.bfloat16),
            pltpu.SemaphoreType.DMA((3,)),
            pltpu.SemaphoreType.DMA((offsets // group,)),
        ],
        compiler_params=pltpu.CompilerParams(vmem_limit_bytes=56 << 20),
    )(pair_table, panels, jnp.asarray(lag), stack_in)


def solution(mesh):
    in_specs = (
        P(("parts", "row"), None, None),
        P(("parts", "row"), None),
        P(("parts", "row"), None),
        P(("parts", "row"), None, None, None, None),
    )
    out_specs = P(("parts", "row"), None, None, None, None)
    return jax.shard_map(shards, mesh=mesh, in_specs=in_specs, out_specs=out_specs, check_vma=False)
```

```python
import functools
import math

import jax
import jax.numpy as jnp
import ml_dtypes
import numpy as np
from jax import lax
from jax.experimental import pallas as pl
from jax.experimental.pallas import tpu as pltpu
from jax.sharding import PartitionSpec as P

SAMPLES = 12000
FLO = 6
BINS = 595
HALF = 40
LAGS = 401
EPSILON = 1e-06

LANE = 128
BLOCKS = -(-BINS // LANE)
WIDTH = BLOCKS * LANE
CHUNK = 256
CHUNKS = -(-SAMPLES // CHUNK)
LAGS_PAD = 512
TALL_BYTES = 10 << 20

MESH = pl.DeviceIdType.MESH


def waves(steps):
    freq = FLO + np.arange(BINS, dtype=np.int64)
    angle = (steps[:, None] * freq[None, :] % SAMPLES) * (2.0 * math.pi / SAMPLES)
    pad = ((0, 0), (0, WIDTH - BINS))
    return np.pad(np.cos(angle), pad), np.pad(-np.sin(angle), pad)


def interleave(real_part, imag_part):
    rows = real_part.shape[0]
    both = np.stack(
        [real_part.reshape(rows, BLOCKS, LANE), imag_part.reshape(rows, BLOCKS, LANE)], axis=2
    )
    return both.reshape(rows, 2 * WIDTH)


def tables():
    dft = interleave(*waves(np.arange(CHUNK, dtype=np.int64))).astype(ml_dtypes.bfloat16)
    turn_real, turn_imag = waves(CHUNK * np.arange(CHUNKS, dtype=np.int64))
    spots = np.arange(WIDTH)
    low, high = np.maximum(spots - HALF, 0), np.minimum(spots + HALF, BINS - 1)
    counts = np.maximum(high - low + 1, 1)[None]
    turns = np.concatenate([turn_real, turn_imag, 1.0 / counts], axis=0)
    turns = np.pad(turns, ((0, -turns.shape[0] % 8), (0, 0))).astype(np.float32)
    lag_real, lag_imag = waves(np.arange(LAGS, dtype=np.int64) - (LAGS - 1) // 2)
    lag = np.pad(interleave(lag_real, lag_imag).T, ((0, 0), (0, LAGS_PAD - LAGS)))
    return dft, turns, lag.astype(ml_dtypes.bfloat16)


def tall(table):
    rows = TALL_BYTES // (table.shape[1] * table.dtype.itemsize)
    return np.pad(table, ((0, rows - table.shape[0]), (0, 0)))


def spectrum_of(x_ref, dft_ref, turns_ref):
    pieces = []
    rows = x_ref.shape[0]
    for chunk in range(CHUNKS):
        first = chunk * CHUNK
        last = min(first + CHUNK, SAMPLES)
        piece = x_ref[:, first:last]
        if last - first < CHUNK:
            blank = jnp.zeros((rows, CHUNK - (last - first)), piece.dtype)
            piece = jnp.concatenate([piece, blank], axis=1)
        pieces.append(piece)
    signal = jnp.concatenate(pieces, axis=0)
    result = []
    for block in range(BLOCKS):
        lanes = slice(2 * LANE * block, 2 * LANE * (block + 1))
        part = jnp.dot(signal, dft_ref[:, lanes], preferred_element_type=jnp.float32)
        bins = slice(LANE * block, LANE * (block + 1))
        real_part = jnp.zeros((rows, LANE), jnp.float32)
        imag_part = jnp.zeros((rows, LANE), jnp.float32)
        for chunk in range(CHUNKS):
            own = part[rows * chunk : rows * (chunk + 1)]
            turn_real = turns_ref[chunk : chunk + 1, bins]
            turn_imag = turns_ref[CHUNKS + chunk : CHUNKS + chunk + 1, bins]
            real_part = real_part + (own[:, :LANE] * turn_real - own[:, LANE:] * turn_imag)
            imag_part = imag_part + (own[:, :LANE] * turn_imag + own[:, LANE:] * turn_real)
        result.append((real_part, imag_part))
    return result


def flag_column(mask_ref, rows):
    segs, chans = mask_ref.shape
    place = lax.broadcasted_iota(jnp.int32, (rows, LANE), 0)
    column = jnp.zeros((rows, LANE), jnp.float32)
    for seg in range(segs):
        for chan in range(chans):
            flag = mask_ref[seg, chan].astype(jnp.float32)
            column = jnp.where(place == seg * chans + chan, flag, column)
    return column


def whitened_blocks(mask_ref, x_ref, dft_ref, turns_ref, band_ref):
    rows = x_ref.shape[0]
    spectrum = spectrum_of(x_ref, dft_ref, turns_ref)
    power = jnp.concatenate([re * re + im * im for re, im in spectrum], axis=1)
    high = power.astype(jnp.bfloat16)
    low = (power - high.astype(jnp.float32)).astype(jnp.bfloat16)
    sums = jnp.dot(
        jnp.concatenate([high, low], axis=0), band_ref[...], preferred_element_type=jnp.float32
    )
    smooth = (sums[:rows] + sums[rows:]) * turns_ref[2 * CHUNKS : 2 * CHUNKS + 1]
    flags = flag_column(mask_ref, rows)
    scale = lax.rsqrt(smooth + EPSILON)
    result = []
    for block, (re, im) in enumerate(spectrum):
        factor = scale[:, LANE * block : LANE * (block + 1)] * flags
        real_part, imag_part = re * factor, im * factor
        if block == BLOCKS - 1:
            lane = lax.broadcasted_iota(jnp.int32, (rows, LANE), 1)
            real_part = jnp.where(lane == LANE - 1, flags, real_part)
        result.append((real_part, imag_part))
    return result


def exchange(
    panel_count, reach, mask_ref, x_ref, dft_hbm, turns_hbm,
    out_ref, dft_ref, turns_ref, band_ref, load_sem, send_sem, forward_sem, recv_sem,
):
    loads = [
        pltpu.make_async_copy(dft_hbm.at[pl.ds(0, CHUNK)], dft_ref, load_sem.at[0]),
        pltpu.make_async_copy(turns_hbm.at[pl.ds(0, turns_ref.shape[0])], turns_ref, load_sem.at[1]),
    ]
    for load in loads:
        load.start()

    me = lax.axis_index("row")
    chips = panel_count // 2
    chip = me // 2
    core = lax.rem(me, 2)
    sibling = {"row": 2 * chip + 1 - core}

    def same_core(offset):
        return {"row": 2 * lax.rem(chip + offset + chips, chips) + core}

    barrier = pltpu.get_barrier_semaphore()
    for offset in range(1, chips):
        pl.semaphore_signal(barrier, inc=1, device_id=same_core(offset), device_id_type=MESH)
    pl.semaphore_signal(barrier, inc=1, device_id=sibling, device_id_type=MESH)

    for block in range(BLOCKS):
        shape = (WIDTH, LANE)
        gap = lax.broadcasted_iota(jnp.int32, shape, 0) - lax.broadcasted_iota(jnp.int32, shape, 1)
        near = jnp.abs(gap - LANE * block) <= HALF
        band_ref[:, LANE * block : LANE * (block + 1)] = jnp.where(near, 1.0, 0.0).astype(
            jnp.bfloat16
        )
    for load in loads:
        load.wait()
    blocks = whitened_blocks(mask_ref, x_ref, dft_ref, turns_ref, band_ref)
    own = core + 1
    for block, (re, im) in enumerate(blocks):
        first = 2 * LANE * block
        out_ref[own, :, first : first + LANE] = re.astype(jnp.bfloat16)
        out_ref[own, :, first + LANE : first + 2 * LANE] = im.astype(jnp.bfloat16)

    pl.semaphore_wait(barrier, chips)

    def copy(source, target, sem, device):
        return pltpu.make_async_remote_copy(
            src_ref=out_ref.at[source],
            dst_ref=out_ref.at[target],
            send_sem=sem,
            recv_sem=recv_sem.at[target],
            device_id=device,
            device_id_type=MESH,
        )

    direct = [
        copy(own, 2 * step + core + 1, send_sem.at[step + 1], same_core(-step))
        for step in range(reach, 0, -1)
    ]
    back = copy(own, 0, send_sem.at[0], same_core(1))
    beside = copy(own, own, send_sem.at[1], sibling)
    for sent in direct:
        sent.start()

    @pl.when(core == 1)
    def _():
        back.start()

    beside.start()

    forwards = []
    back_forward = copy(0, 0, forward_sem.at[0], sibling)
    for step in range(1, reach + 1):
        slot = 2 * step + core + 1
        passed = copy(slot, slot, forward_sem.at[step], sibling)
        passed.wait_recv()
        passed.start()
        forwards.append(passed)
        if step == 1:

            @pl.when(core == 1)
            def _():
                back_forward.wait_recv()
                back_forward.start()

    copy(2 - core, 2 - core, send_sem.at[1], sibling).wait_recv()
    for step in range(1, reach + 1):
        slot = 2 * step + 2 - core
        copy(slot, slot, forward_sem.at[step], sibling).wait_recv()

    @pl.when(core == 0)
    def _():
        back_forward.wait_recv()

    for sent in direct + [beside] + forwards:
        sent.wait_send()

    @pl.when(core == 1)
    def _():
        back.wait_send()
        back_forward.wait_send()


def correlate(panel_count, pair_ref, panels_ref, lag_ref, stack_ref, out_ref, cross_ref):
    me = lax.axis_index("row")
    core = lax.rem(me, 2)
    first = me - core - 1
    step = pl.program_id(0)
    slots = stack_ref.shape[1]
    chans = stack_ref.shape[2]
    own = panels_ref[core + 1].astype(jnp.float32)
    segs = own.shape[0] // chans
    for slot in range(slots):
        panel = pair_ref[0, step * slots + slot]
        place = lax.rem(panel - first + panel_count, panel_count)
        partner = panels_ref[place].astype(jnp.float32)
        for chan in range(chans):
            scale = None
            for block in range(BLOCKS - 1, -1, -1):
                at = 2 * LANE * block
                re = im = 0.0
                for seg in range(segs):
                    mine = own[seg * chans + chan : seg * chans + chan + 1]
                    other = partner[seg * chans : (seg + 1) * chans]
                    own_re, own_im = mine[:, at : at + LANE], mine[:, at + LANE : at + 2 * LANE]
                    part_re, part_im = other[:, at : at + LANE], other[:, at + LANE : at + 2 * LANE]
                    re = re + (own_re * part_re + own_im * part_im)
                    im = im + (own_im * part_re - own_re * part_im)
                if scale is None:
                    count = re[:, LANE - 1 : LANE]
                    scale = 1.0 / jnp.maximum(count, 1.0)
                row = (slot * chans + chan) * chans
                cross_ref[row : row + chans, at : at + LANE] = (re * scale).astype(jnp.bfloat16)
                cross_ref[row : row + chans, at + LANE : at + 2 * LANE] = (im * scale).astype(
                    jnp.bfloat16
                )
    corr = jnp.dot(cross_ref[...], lag_ref[...], preferred_element_type=jnp.float32)
    corr = corr[:, :LAGS] * (1.0 / math.sqrt(BINS))
    out_ref[...] = stack_ref[...] + corr.reshape(stack_ref.shape)


def shards(traces, valid_mask, pair_table, stack_in):
    panel_count = lax.axis_size("row")
    chans, segs, samples = traces.shape
    rows = chans * segs
    offsets = pair_table.shape[1]
    reach = (offsets - 2) // 2
    dft, turns, lag = tables()
    x = jnp.transpose(traces, (1, 0, 2)).reshape(rows, samples)
    vmem = pl.BlockSpec(memory_space=pltpu.VMEM)
    hbm = pl.BlockSpec(memory_space=pltpu.HBM)
    smem = pl.BlockSpec(memory_space=pltpu.SMEM)
    panels = pl.pallas_call(
        functools.partial(exchange, panel_count, reach),
        out_shape=jax.ShapeDtypeStruct((offsets + 1, rows, 2 * WIDTH), jnp.bfloat16),
        in_specs=[smem, vmem, hbm, hbm],
        out_specs=vmem,
        scratch_shapes=[
            pltpu.VMEM(dft.shape, jnp.bfloat16),
            pltpu.VMEM(turns.shape, jnp.float32),
            pltpu.VMEM((WIDTH, WIDTH), jnp.bfloat16),
            pltpu.SemaphoreType.DMA((2,)),
            pltpu.SemaphoreType.DMA((reach + 2,)),
            pltpu.SemaphoreType.DMA((reach + 2,)),
            pltpu.SemaphoreType.DMA((offsets + 1,)),
        ],
        compiler_params=pltpu.CompilerParams(
            collective_id=0, has_side_effects=True, vmem_limit_bytes=50 << 20
        ),
    )(valid_mask.T, x, jnp.asarray(tall(dft)), jnp.asarray(tall(turns)))
    group = max(size for size in range(1, 7) if offsets % size == 0)
    tile = (1, group, chans, chans, stack_in.shape[4])
    return pl.pallas_call(
        functools.partial(correlate, panel_count),
        out_shape=jax.ShapeDtypeStruct(stack_in.shape, stack_in.dtype),
        grid_spec=pltpu.PrefetchScalarGridSpec(
            num_scalar_prefetch=1,
            grid=(offsets // group,),
            in_specs=[
                pl.BlockSpec(panels.shape, lambda i, pair: (0, 0, 0)),
                pl.BlockSpec(lag.shape, lambda i, pair: (0, 0)),
                pl.BlockSpec(tile, lambda i, pair: (0, i, 0, 0, 0)),
            ],
            out_specs=pl.BlockSpec(tile, lambda i, pair: (0, i, 0, 0, 0)),
            scratch_shapes=[pltpu.VMEM((group * chans * chans, 2 * WIDTH), jnp.bfloat16)],
        ),
        compiler_params=pltpu.CompilerParams(vmem_limit_bytes=32 << 20),
    )(pair_table, panels, jnp.asarray(lag), stack_in)


def solution(mesh):
    in_specs = (
        P(("parts", "row"), None, None),
        P(("parts", "row"), None),
        P(("parts", "row"), None),
        P(("parts", "row"), None, None, None, None),
    )
    out_specs = P(("parts", "row"), None, None, None, None)
    return jax.shard_map(shards, mesh=mesh, in_specs=in_specs, out_specs=out_specs, check_vma=False)
```

```python
import functools
import math

import jax
import jax.numpy as jnp
import ml_dtypes
import numpy as np
from jax import lax
from jax.experimental import pallas as pl
from jax.experimental.pallas import tpu as pltpu
from jax.sharding import PartitionSpec as P

SAMPLES = 12000
FLO = 6
BINS = 595
HALF = 40
LAGS = 401
EPSILON = 1e-06

LANE = 128
BLOCKS = -(-BINS // LANE)
WIDTH = BLOCKS * LANE
CHUNK = 256
CHUNKS = -(-SAMPLES // CHUNK)
LAGS_PAD = 512
TALL_BYTES = 10 << 20

MESH = pl.DeviceIdType.MESH


def waves(steps):
    freq = FLO + np.arange(BINS, dtype=np.int64)
    angle = (steps[:, None] * freq[None, :] % SAMPLES) * (2.0 * math.pi / SAMPLES)
    pad = ((0, 0), (0, WIDTH - BINS))
    return np.pad(np.cos(angle), pad), np.pad(-np.sin(angle), pad)


def interleave(real_part, imag_part):
    rows = real_part.shape[0]
    both = np.stack(
        [real_part.reshape(rows, BLOCKS, LANE), imag_part.reshape(rows, BLOCKS, LANE)], axis=2
    )
    return both.reshape(rows, 2 * WIDTH)


def tables():
    dft = interleave(*waves(np.arange(CHUNK, dtype=np.int64))).astype(ml_dtypes.bfloat16)
    turn_real, turn_imag = waves(CHUNK * np.arange(CHUNKS, dtype=np.int64))
    spots = np.arange(WIDTH)
    low, high = np.maximum(spots - HALF, 0), np.minimum(spots + HALF, BINS - 1)
    counts = np.maximum(high - low + 1, 1)[None]
    turns = np.concatenate([turn_real, turn_imag, 1.0 / counts], axis=0)
    turns = np.pad(turns, ((0, -turns.shape[0] % 8), (0, 0))).astype(np.float32)
    lag_real, lag_imag = waves(np.arange(LAGS, dtype=np.int64) - (LAGS - 1) // 2)
    lag = np.pad(interleave(lag_real, lag_imag).T, ((0, 0), (0, LAGS_PAD - LAGS)))
    return dft, turns, lag.astype(ml_dtypes.bfloat16)


def tall(table):
    rows = TALL_BYTES // (table.shape[1] * table.dtype.itemsize)
    return np.pad(table, ((0, rows - table.shape[0]), (0, 0)))


def spectrum_of(x_ref, dft_ref, turns_ref):
    pieces = []
    rows = x_ref.shape[0]
    for chunk in range(CHUNKS):
        first = chunk * CHUNK
        last = min(first + CHUNK, SAMPLES)
        piece = x_ref[:, first:last]
        if last - first < CHUNK:
            blank = jnp.zeros((rows, CHUNK - (last - first)), piece.dtype)
            piece = jnp.concatenate([piece, blank], axis=1)
        pieces.append(piece)
    signal = jnp.concatenate(pieces, axis=0)
    result = []
    for block in range(BLOCKS):
        lanes = slice(2 * LANE * block, 2 * LANE * (block + 1))
        part = jnp.dot(signal, dft_ref[:, lanes], preferred_element_type=jnp.float32)
        bins = slice(LANE * block, LANE * (block + 1))
        real_part = jnp.zeros((rows, LANE), jnp.float32)
        imag_part = jnp.zeros((rows, LANE), jnp.float32)
        for chunk in range(CHUNKS):
            own = part[rows * chunk : rows * (chunk + 1)]
            turn_real = turns_ref[chunk : chunk + 1, bins]
            turn_imag = turns_ref[CHUNKS + chunk : CHUNKS + chunk + 1, bins]
            real_part = real_part + (own[:, :LANE] * turn_real - own[:, LANE:] * turn_imag)
            imag_part = imag_part + (own[:, :LANE] * turn_imag + own[:, LANE:] * turn_real)
        result.append((real_part, imag_part))
    return result


def flag_column(mask_ref, rows):
    segs, chans = mask_ref.shape
    place = lax.broadcasted_iota(jnp.int32, (rows, LANE), 0)
    column = jnp.zeros((rows, LANE), jnp.float32)
    for seg in range(segs):
        for chan in range(chans):
            flag = mask_ref[seg, chan].astype(jnp.float32)
            column = jnp.where(place == seg * chans + chan, flag, column)
    return column


def whitened_blocks(mask_ref, x_ref, dft_ref, turns_ref, band_ref):
    rows = x_ref.shape[0]
    spectrum = spectrum_of(x_ref, dft_ref, turns_ref)
    power = jnp.concatenate([re * re + im * im for re, im in spectrum], axis=1)
    high = power.astype(jnp.bfloat16)
    low = (power - high.astype(jnp.float32)).astype(jnp.bfloat16)
    sums = jnp.dot(
        jnp.concatenate([high, low], axis=0), band_ref[...], preferred_element_type=jnp.float32
    )
    smooth = (sums[:rows] + sums[rows:]) * turns_ref[2 * CHUNKS : 2 * CHUNKS + 1]
    flags = flag_column(mask_ref, rows)
    scale = lax.rsqrt(smooth + EPSILON)
    result = []
    for block, (re, im) in enumerate(spectrum):
        factor = scale[:, LANE * block : LANE * (block + 1)] * flags
        real_part, imag_part = re * factor, im * factor
        if block == BLOCKS - 1:
            lane = lax.broadcasted_iota(jnp.int32, (rows, LANE), 1)
            real_part = jnp.where(lane == LANE - 1, flags, real_part)
        result.append((real_part, imag_part))
    return result


def exchange(
    panel_count, reach, mask_ref, x_ref, dft_hbm, turns_hbm,
    out_ref, dft_ref, turns_ref, band_ref, load_sem, send_sem,
    column_sem, relay_sem, forward_sem, recv_sem,
):
    loads = [
        pltpu.make_async_copy(dft_hbm.at[pl.ds(0, CHUNK)], dft_ref, load_sem.at[0]),
        pltpu.make_async_copy(turns_hbm.at[pl.ds(0, turns_ref.shape[0])], turns_ref, load_sem.at[1]),
    ]
    for load in loads:
        load.start()

    me = lax.axis_index("row")
    chips = panel_count // 2
    chip = me // 2
    core = lax.rem(me, 2)
    sibling = {"row": 2 * chip + 1 - core}

    def same_core(offset):
        return {"row": 2 * lax.rem(chip + offset + chips, chips) + core}

    barrier = pltpu.get_barrier_semaphore()
    for offset in range(1, chips):
        pl.semaphore_signal(barrier, inc=1, device_id=same_core(offset), device_id_type=MESH)
    pl.semaphore_signal(barrier, inc=1, device_id=sibling, device_id_type=MESH)

    for block in range(BLOCKS):
        shape = (WIDTH, LANE)
        gap = lax.broadcasted_iota(jnp.int32, shape, 0) - lax.broadcasted_iota(jnp.int32, shape, 1)
        near = jnp.abs(gap - LANE * block) <= HALF
        band_ref[:, LANE * block : LANE * (block + 1)] = jnp.where(near, 1.0, 0.0).astype(
            jnp.bfloat16
        )
    for load in loads:
        load.wait()
    blocks = whitened_blocks(mask_ref, x_ref, dft_ref, turns_ref, band_ref)
    own = core + 1
    for block, (re, im) in enumerate(blocks):
        first = 2 * LANE * block
        out_ref[own, :, first : first + LANE] = re.astype(jnp.bfloat16)
        out_ref[own, :, first + LANE : first + 2 * LANE] = im.astype(jnp.bfloat16)

    pl.semaphore_wait(barrier, chips)

    def copy(source, target, sem, device):
        return pltpu.make_async_remote_copy(
            src_ref=out_ref.at[source],
            dst_ref=out_ref.at[target],
            send_sem=sem,
            recv_sem=recv_sem.at[target],
            device_id=device,
            device_id_type=MESH,
        )

    side = lax.rem(chip, 2)
    partner = {"row": 2 * (chip + 1 - 2 * side) + core}
    nodes = reach // 2
    columns = [
        copy(own, 4 * step + core + 1, column_sem.at[step - 1], same_core(-2 * step))
        for step in range(1, nodes + 1)
    ]

    def relay(step):
        target = 4 * step - 1 + core
        return copy(4 * (step - side) + core + 1, target, relay_sem.at[step - 1], partner)

    def forward(slot, step):
        return copy(slot, slot, forward_sem.at[step], sibling)

    back = copy(own, 0, send_sem.at[0], same_core(1))
    beside = copy(own, own, send_sem.at[1], sibling)
    for sent in columns:
        sent.start()

    @pl.when(side == 1)
    def _():
        relay(1).start()

    @pl.when(core == 1)
    def _():
        back.start()

    beside.start()

    for step in range(1, nodes + 1):
        passed = forward(4 * step + core + 1, 2 * step)
        passed.wait_recv()
        if step < nodes:
            relay(step + side).start()
        else:

            @pl.when(side == 0)
            def _():
                relay(nodes).start()

        passed.start()
    for step in range(1, nodes + 1):
        passed = forward(4 * step - 1 + core, 2 * step - 1)
        passed.wait_recv()
        passed.start()

    @pl.when(core == 1)
    def _():
        forward(0, 0).wait_recv()
        forward(0, 0).start()

    copy(2 - core, 2 - core, send_sem.at[1], sibling).wait_recv()
    for step in range(1, reach + 1):
        forward(2 * step + 2 - core, step).wait_recv()

    @pl.when(core == 0)
    def _():
        forward(0, 0).wait_recv()

    for sent in columns + [beside]:
        sent.wait_send()
    for step in range(1, nodes + 1):
        relay(step).wait_send()
    for step in range(1, reach + 1):
        forward(own, step).wait_send()

    @pl.when(core == 1)
    def _():
        back.wait_send()
        forward(0, 0).wait_send()


def correlate(panel_count, pair_ref, panels_ref, lag_ref, stack_ref, out_ref, cross_ref):
    me = lax.axis_index("row")
    core = lax.rem(me, 2)
    first = me - core - 1
    step = pl.program_id(0)
    slots = stack_ref.shape[1]
    chans = stack_ref.shape[2]
    own = panels_ref[core + 1].astype(jnp.float32)
    segs = own.shape[0] // chans
    for slot in range(slots):
        panel = pair_ref[0, step * slots + slot]
        place = lax.rem(panel - first + panel_count, panel_count)
        partner = panels_ref[place].astype(jnp.float32)
        for chan in range(chans):
            scale = None
            for block in range(BLOCKS - 1, -1, -1):
                at = 2 * LANE * block
                re = im = 0.0
                for seg in range(segs):
                    mine = own[seg * chans + chan : seg * chans + chan + 1]
                    other = partner[seg * chans : (seg + 1) * chans]
                    own_re, own_im = mine[:, at : at + LANE], mine[:, at + LANE : at + 2 * LANE]
                    part_re, part_im = other[:, at : at + LANE], other[:, at + LANE : at + 2 * LANE]
                    re = re + (own_re * part_re + own_im * part_im)
                    im = im + (own_im * part_re - own_re * part_im)
                if scale is None:
                    count = re[:, LANE - 1 : LANE]
                    scale = 1.0 / jnp.maximum(count, 1.0)
                row = (slot * chans + chan) * chans
                cross_ref[row : row + chans, at : at + LANE] = (re * scale).astype(jnp.bfloat16)
                cross_ref[row : row + chans, at + LANE : at + 2 * LANE] = (im * scale).astype(
                    jnp.bfloat16
                )
    corr = jnp.dot(cross_ref[...], lag_ref[...], preferred_element_type=jnp.float32)
    corr = corr[:, :LAGS] * (1.0 / math.sqrt(BINS))
    out_ref[...] = stack_ref[...] + corr.reshape(stack_ref.shape)


def shards(traces, valid_mask, pair_table, stack_in):
    panel_count = lax.axis_size("row")
    chans, segs, samples = traces.shape
    rows = chans * segs
    offsets = pair_table.shape[1]
    reach = (offsets - 2) // 2
    dft, turns, lag = tables()
    x = jnp.transpose(traces, (1, 0, 2)).reshape(rows, samples)
    vmem = pl.BlockSpec(memory_space=pltpu.VMEM)
    hbm = pl.BlockSpec(memory_space=pltpu.HBM)
    smem = pl.BlockSpec(memory_space=pltpu.SMEM)
    panels = pl.pallas_call(
        functools.partial(exchange, panel_count, reach),
        out_shape=jax.ShapeDtypeStruct((offsets + 1, rows, 2 * WIDTH), jnp.bfloat16),
        in_specs=[smem, vmem, hbm, hbm],
        out_specs=vmem,
        scratch_shapes=[
            pltpu.VMEM(dft.shape, jnp.bfloat16),
            pltpu.VMEM(turns.shape, jnp.float32),
            pltpu.VMEM((WIDTH, WIDTH), jnp.bfloat16),
            pltpu.SemaphoreType.DMA((2,)),
            pltpu.SemaphoreType.DMA((2,)),
            pltpu.SemaphoreType.DMA((reach // 2,)),
            pltpu.SemaphoreType.DMA((reach // 2,)),
            pltpu.SemaphoreType.DMA((reach + 1,)),
            pltpu.SemaphoreType.DMA((offsets + 1,)),
        ],
        compiler_params=pltpu.CompilerParams(
            collective_id=0, has_side_effects=True, vmem_limit_bytes=50 << 20
        ),
    )(valid_mask.T, x, jnp.asarray(tall(dft)), jnp.asarray(tall(turns)))
    group = max(size for size in range(1, 7) if offsets % size == 0)
    tile = (1, group, chans, chans, stack_in.shape[4])
    return pl.pallas_call(
        functools.partial(correlate, panel_count),
        out_shape=jax.ShapeDtypeStruct(stack_in.shape, stack_in.dtype),
        grid_spec=pltpu.PrefetchScalarGridSpec(
            num_scalar_prefetch=1,
            grid=(offsets // group,),
            in_specs=[
                pl.BlockSpec(panels.shape, lambda i, pair: (0, 0, 0)),
                pl.BlockSpec(lag.shape, lambda i, pair: (0, 0)),
                pl.BlockSpec(tile, lambda i, pair: (0, i, 0, 0, 0)),
            ],
            out_specs=pl.BlockSpec(tile, lambda i, pair: (0, i, 0, 0, 0)),
            scratch_shapes=[pltpu.VMEM((group * chans * chans, 2 * WIDTH), jnp.bfloat16)],
        ),
        compiler_params=pltpu.CompilerParams(vmem_limit_bytes=32 << 20),
    )(pair_table, panels, jnp.asarray(lag), stack_in)


def solution(mesh):
    in_specs = (
        P(("parts", "row"), None, None),
        P(("parts", "row"), None),
        P(("parts", "row"), None),
        P(("parts", "row"), None, None, None, None),
    )
    out_specs = P(("parts", "row"), None, None, None, None)
    return jax.shard_map(shards, mesh=mesh, in_specs=in_specs, out_specs=out_specs, check_vma=False)
```

```python
import functools
import math

import jax
import jax.numpy as jnp
import ml_dtypes
import numpy as np
from jax import lax
from jax.experimental import pallas as pl
from jax.experimental.pallas import tpu as pltpu
from jax.sharding import PartitionSpec as P

SAMPLES = 12000
FLO = 6
BINS = 595
HALF = 40
LAGS = 401
EPSILON = 1e-06

LANE = 128
BLOCKS = -(-BINS // LANE)
WIDTH = BLOCKS * LANE
CHUNK = 256
CHUNKS = -(-SAMPLES // CHUNK)
LAGS_PAD = 512
TALL_BYTES = 10 << 20
LOADS = 4

MESH = pl.DeviceIdType.MESH


def waves(steps):
    freq = FLO + np.arange(BINS, dtype=np.int64)
    angle = (steps[:, None] * freq[None, :] % SAMPLES) * (2.0 * math.pi / SAMPLES)
    pad = ((0, 0), (0, WIDTH - BINS))
    return np.pad(np.cos(angle), pad), np.pad(-np.sin(angle), pad)


def interleave(real_part, imag_part):
    rows = real_part.shape[0]
    both = np.stack(
        [real_part.reshape(rows, BLOCKS, LANE), imag_part.reshape(rows, BLOCKS, LANE)], axis=2
    )
    return both.reshape(rows, 2 * WIDTH)


def tables():
    dft = interleave(*waves(np.arange(CHUNK, dtype=np.int64))).astype(ml_dtypes.bfloat16)
    turn_real, turn_imag = waves(CHUNK * np.arange(CHUNKS, dtype=np.int64))
    spots = np.arange(WIDTH)
    low, high = np.maximum(spots - HALF, 0), np.minimum(spots + HALF, BINS - 1)
    counts = np.maximum(high - low + 1, 1)[None]
    turns = np.concatenate([turn_real, turn_imag, 1.0 / counts], axis=0)
    turns = np.pad(turns, ((0, -turns.shape[0] % 8), (0, 0))).astype(np.float32)
    lag_real, lag_imag = waves(np.arange(LAGS, dtype=np.int64) - (LAGS - 1) // 2)
    lag = np.pad(interleave(lag_real, lag_imag).T, ((0, 0), (0, LAGS_PAD - LAGS)))
    return dft, turns, lag.astype(ml_dtypes.bfloat16)


def tall(table):
    rows = TALL_BYTES // (table.shape[1] * table.dtype.itemsize)
    return np.pad(table, ((0, rows - table.shape[0]), (0, 0)))


def spectrum_of(x_ref, dft_ref, turns_ref):
    pieces = []
    rows = x_ref.shape[0]
    for chunk in range(CHUNKS):
        first = chunk * CHUNK
        last = min(first + CHUNK, SAMPLES)
        piece = x_ref[:, first:last]
        if last - first < CHUNK:
            blank = jnp.zeros((rows, CHUNK - (last - first)), piece.dtype)
            piece = jnp.concatenate([piece, blank], axis=1)
        pieces.append(piece)
    signal = jnp.concatenate(pieces, axis=0)
    result = []
    for block in range(BLOCKS):
        lanes = slice(2 * LANE * block, 2 * LANE * (block + 1))
        part = jnp.dot(signal, dft_ref[:, lanes], preferred_element_type=jnp.float32)
        bins = slice(LANE * block, LANE * (block + 1))
        real_part = jnp.zeros((rows, LANE), jnp.float32)
        imag_part = jnp.zeros((rows, LANE), jnp.float32)
        for chunk in range(CHUNKS):
            own = part[rows * chunk : rows * (chunk + 1)]
            turn_real = turns_ref[chunk : chunk + 1, bins]
            turn_imag = turns_ref[CHUNKS + chunk : CHUNKS + chunk + 1, bins]
            real_part = real_part + (own[:, :LANE] * turn_real - own[:, LANE:] * turn_imag)
            imag_part = imag_part + (own[:, :LANE] * turn_imag + own[:, LANE:] * turn_real)
        result.append((real_part, imag_part))
    return result


def flag_column(mask_ref, rows):
    segs, chans = mask_ref.shape
    place = lax.broadcasted_iota(jnp.int32, (rows, LANE), 0)
    column = jnp.zeros((rows, LANE), jnp.float32)
    for seg in range(segs):
        for chan in range(chans):
            flag = mask_ref[seg, chan].astype(jnp.float32)
            column = jnp.where(place == seg * chans + chan, flag, column)
    return column


def whitened_blocks(mask_ref, x_ref, dft_ref, turns_ref, band_ref):
    rows = x_ref.shape[0]
    spectrum = spectrum_of(x_ref, dft_ref, turns_ref)
    power = jnp.concatenate([re * re + im * im for re, im in spectrum], axis=1)
    high = power.astype(jnp.bfloat16)
    low = (power - high.astype(jnp.float32)).astype(jnp.bfloat16)
    sums = jnp.dot(
        jnp.concatenate([high, low], axis=0), band_ref[...], preferred_element_type=jnp.float32
    )
    smooth = (sums[:rows] + sums[rows:]) * turns_ref[2 * CHUNKS : 2 * CHUNKS + 1]
    flags = flag_column(mask_ref, rows)
    scale = lax.rsqrt(smooth + EPSILON)
    result = []
    for block, (re, im) in enumerate(spectrum):
        factor = scale[:, LANE * block : LANE * (block + 1)] * flags
        real_part, imag_part = re * factor, im * factor
        if block == BLOCKS - 1:
            lane = lax.broadcasted_iota(jnp.int32, (rows, LANE), 1)
            real_part = jnp.where(lane == LANE - 1, flags, real_part)
        result.append((real_part, imag_part))
    return result


def exchange(
    panel_count, reach, mask_ref, x_ref, dft_hbm, turns_hbm,
    out_ref, dft_ref, turns_ref, band_ref, load_sem, send_sem,
    column_sem, relay_sem, forward_sem, recv_sem,
):
    loads = [
        pltpu.make_async_copy(turns_hbm.at[pl.ds(0, turns_ref.shape[0])], turns_ref, load_sem.at[0])
    ]
    depth = CHUNK // LOADS
    for piece in range(LOADS):
        lines = pl.ds(depth * piece, depth)
        loads.append(
            pltpu.make_async_copy(dft_hbm.at[lines], dft_ref.at[lines], load_sem.at[1 + piece])
        )
    for load in loads:
        load.start()

    me = lax.axis_index("row")
    chips = panel_count // 2
    chip = me // 2
    core = lax.rem(me, 2)
    sibling = {"row": 2 * chip + 1 - core}

    def same_core(offset):
        return {"row": 2 * lax.rem(chip + offset + chips, chips) + core}

    barrier = pltpu.get_barrier_semaphore()
    for offset in range(1, chips):
        pl.semaphore_signal(barrier, inc=1, device_id=same_core(offset), device_id_type=MESH)
    pl.semaphore_signal(barrier, inc=1, device_id=sibling, device_id_type=MESH)

    for block in range(BLOCKS):
        shape = (WIDTH, LANE)
        gap = lax.broadcasted_iota(jnp.int32, shape, 0) - lax.broadcasted_iota(jnp.int32, shape, 1)
        near = jnp.abs(gap - LANE * block) <= HALF
        band_ref[:, LANE * block : LANE * (block + 1)] = jnp.where(near, 1.0, 0.0).astype(
            jnp.bfloat16
        )
    for load in loads:
        load.wait()
    blocks = whitened_blocks(mask_ref, x_ref, dft_ref, turns_ref, band_ref)
    own = core + 1
    for block, (re, im) in enumerate(blocks):
        first = 2 * LANE * block
        out_ref[own, :, first : first + LANE] = re.astype(jnp.bfloat16)
        out_ref[own, :, first + LANE : first + 2 * LANE] = im.astype(jnp.bfloat16)

    pl.semaphore_wait(barrier, chips)

    def copy(source, target, sem, device):
        return pltpu.make_async_remote_copy(
            src_ref=out_ref.at[source],
            dst_ref=out_ref.at[target],
            send_sem=sem,
            recv_sem=recv_sem.at[target],
            device_id=device,
            device_id_type=MESH,
        )

    side = lax.rem(chip, 2)
    partner = {"row": 2 * (chip + 1 - 2 * side) + core}
    nodes = reach // 2
    columns = [
        copy(own, 4 * step + core + 1, column_sem.at[step - 1], same_core(-2 * step))
        for step in range(1, nodes + 1)
    ]

    def relay(step):
        target = 4 * step - 1 + core
        return copy(4 * (step - side) + core + 1, target, relay_sem.at[step - 1], partner)

    def forward(slot, step):
        return copy(slot, slot, forward_sem.at[step], sibling)

    back = copy(own, 0, send_sem.at[0], same_core(1))
    beside = copy(own, own, send_sem.at[1], sibling)
    for sent in columns:
        sent.start()

    @pl.when(side == 1)
    def _():
        relay(1).start()

    @pl.when(core == 1)
    def _():
        back.start()

    beside.start()

    for step in range(1, nodes + 1):
        passed = forward(4 * step + core + 1, 2 * step)
        passed.wait_recv()
        if step < nodes:
            relay(step + side).start()
        else:

            @pl.when(side == 0)
            def _():
                relay(nodes).start()

        passed.start()
    for step in range(1, nodes + 1):
        passed = forward(4 * step - 1 + core, 2 * step - 1)
        passed.wait_recv()
        passed.start()

    @pl.when(core == 1)
    def _():
        forward(0, 0).wait_recv()
        forward(0, 0).start()

    copy(2 - core, 2 - core, send_sem.at[1], sibling).wait_recv()
    for step in range(1, reach + 1):
        forward(2 * step + 2 - core, step).wait_recv()

    @pl.when(core == 0)
    def _():
        forward(0, 0).wait_recv()

    for sent in columns + [beside]:
        sent.wait_send()
    for step in range(1, nodes + 1):
        relay(step).wait_send()
    for step in range(1, reach + 1):
        forward(own, step).wait_send()

    @pl.when(core == 1)
    def _():
        back.wait_send()
        forward(0, 0).wait_send()


def correlate(panel_count, pair_ref, panels_ref, lag_ref, stack_ref, out_ref, cross_ref):
    me = lax.axis_index("row")
    core = lax.rem(me, 2)
    first = me - core - 1
    step = pl.program_id(0)
    slots = stack_ref.shape[1]
    chans = stack_ref.shape[2]
    own = panels_ref[core + 1].astype(jnp.float32)
    segs = own.shape[0] // chans
    for slot in range(slots):
        panel = pair_ref[0, step * slots + slot]
        place = lax.rem(panel - first + panel_count, panel_count)
        partner = panels_ref[place].astype(jnp.float32)
        for chan in range(chans):
            scale = None
            for block in range(BLOCKS - 1, -1, -1):
                at = 2 * LANE * block
                re = im = 0.0
                for seg in range(segs):
                    mine = own[seg * chans + chan : seg * chans + chan + 1]
                    other = partner[seg * chans : (seg + 1) * chans]
                    own_re, own_im = mine[:, at : at + LANE], mine[:, at + LANE : at + 2 * LANE]
                    part_re, part_im = other[:, at : at + LANE], other[:, at + LANE : at + 2 * LANE]
                    re = re + (own_re * part_re + own_im * part_im)
                    im = im + (own_im * part_re - own_re * part_im)
                if scale is None:
                    count = re[:, LANE - 1 : LANE]
                    scale = 1.0 / jnp.maximum(count, 1.0)
                row = (slot * chans + chan) * chans
                cross_ref[row : row + chans, at : at + LANE] = (re * scale).astype(jnp.bfloat16)
                cross_ref[row : row + chans, at + LANE : at + 2 * LANE] = (im * scale).astype(
                    jnp.bfloat16
                )
    corr = jnp.dot(cross_ref[...], lag_ref[...], preferred_element_type=jnp.float32)
    corr = corr[:, :LAGS] * (1.0 / math.sqrt(BINS))
    out_ref[...] = stack_ref[...] + corr.reshape(stack_ref.shape)


def shards(traces, valid_mask, pair_table, stack_in):
    panel_count = lax.axis_size("row")
    chans, segs, samples = traces.shape
    rows = chans * segs
    offsets = pair_table.shape[1]
    reach = (offsets - 2) // 2
    dft, turns, lag = tables()
    x = jnp.transpose(traces, (1, 0, 2)).reshape(rows, samples)
    vmem = pl.BlockSpec(memory_space=pltpu.VMEM)
    hbm = pl.BlockSpec(memory_space=pltpu.HBM)
    smem = pl.BlockSpec(memory_space=pltpu.SMEM)
    panels = pl.pallas_call(
        functools.partial(exchange, panel_count, reach),
        out_shape=jax.ShapeDtypeStruct((offsets + 1, rows, 2 * WIDTH), jnp.bfloat16),
        in_specs=[smem, vmem, hbm, hbm],
        out_specs=vmem,
        scratch_shapes=[
            pltpu.VMEM(dft.shape, jnp.bfloat16),
            pltpu.VMEM(turns.shape, jnp.float32),
            pltpu.VMEM((WIDTH, WIDTH), jnp.bfloat16),
            pltpu.SemaphoreType.DMA((1 + LOADS,)),
            pltpu.SemaphoreType.DMA((2,)),
            pltpu.SemaphoreType.DMA((reach // 2,)),
            pltpu.SemaphoreType.DMA((reach // 2,)),
            pltpu.SemaphoreType.DMA((reach + 1,)),
            pltpu.SemaphoreType.DMA((offsets + 1,)),
        ],
        compiler_params=pltpu.CompilerParams(
            collective_id=0, has_side_effects=True, vmem_limit_bytes=50 << 20
        ),
    )(valid_mask.T, x, jnp.asarray(tall(dft)), jnp.asarray(tall(turns)))
    group = max(size for size in range(1, 7) if offsets % size == 0)
    tile = (1, group, chans, chans, stack_in.shape[4])
    return pl.pallas_call(
        functools.partial(correlate, panel_count),
        out_shape=jax.ShapeDtypeStruct(stack_in.shape, stack_in.dtype),
        grid_spec=pltpu.PrefetchScalarGridSpec(
            num_scalar_prefetch=1,
            grid=(offsets // group,),
            in_specs=[
                pl.BlockSpec(panels.shape, lambda i, pair: (0, 0, 0)),
                pl.BlockSpec(lag.shape, lambda i, pair: (0, 0)),
                pl.BlockSpec(tile, lambda i, pair: (0, i, 0, 0, 0)),
            ],
            out_specs=pl.BlockSpec(tile, lambda i, pair: (0, i, 0, 0, 0)),
            scratch_shapes=[pltpu.VMEM((group * chans * chans, 2 * WIDTH), jnp.bfloat16)],
        ),
        compiler_params=pltpu.CompilerParams(vmem_limit_bytes=32 << 20),
    )(pair_table, panels, jnp.asarray(lag), stack_in)


def solution(mesh):
    in_specs = (
        P(("parts", "row"), None, None),
        P(("parts", "row"), None),
        P(("parts", "row"), None),
        P(("parts", "row"), None, None, None, None),
    )
    out_specs = P(("parts", "row"), None, None, None, None)
    return jax.shard_map(shards, mesh=mesh, in_specs=in_specs, out_specs=out_specs, check_vma=False)
```
